512 devices in a mesh: gx: 16 (over y, core), gy: 8 (over z_hi, x), gz: 4 (over z_lo).
Axes of the slice: x: 4, y: 8, z: 8 (z_hi: 2, z_lo: 4; z = z_hi * 4 + z_lo), core: 2. Of those that a mesh axis runs over, the one named last changes fastest.
Arguments:
- adjoint_final: float32 [3, 512, 64, 512], P(None, 'gx', 'gy', 'gz'), may hold values from -6 to 6
- velocity: float32 [3, 512, 64, 512], P(None, ('gx', 'gy', 'gz')), may hold values from -0.15 to 0.15
- diffusivity: float32 [3, 512, 64, 512], P(None, 'gx', 'gy', 'gz'), may hold values from 0.01 to 0.04
- upwind_side: int32 [3, 512, 64, 512], P(None, 'gx', 'gy', 'gz'), may hold values 0 or 1
- wall_mask: int32 [512, 64, 512], P('gx', 'gy', 'gz'), may hold values 0 or 1
Outputs:
- adjoint_initial: float32 [3, 512, 64, 512], P(None, 'gx', 'gy', 'gz')
The draws below stay inside these ranges and needn't reach their ends.
All inputs are finite; a program needn't handle non-finite values. No bound on the sum of `upwind_side` or of `wall_mask` on one device may be relied on, other than what follows from the above.
Results may differ from the reference program's by a relative error of at most 0.00002.
Values sent between devices are 32-bit elements; how exact they have to be, the bound alone decides.
A program may use at most 128 MiB of HBM per device.

```python
import math
import jax
import jax.numpy as jnp
from jax import lax

SOLUTES = 3
STEPS = 5
NX = 512
NY = 64
NZ = 512


def with_ends(entries, own_key, smallest, top_value):
    index_at = [jax.random.randint(jax.random.fold_in(own_key, axis), (), 0, length) for axis, length in enumerate(entries.shape)]
    longest = entries.shape.index(max(entries.shape))
    neighbour = index_at[:longest] + [(index_at[longest] + 1) % entries.shape[longest]] + index_at[longest + 1:]
    return entries.at[tuple(index_at)].set(smallest).at[tuple(neighbour)].set(top_value)


def levels(rng, shape, split, low, top_value):
    gain, own = 1.0, jax.random.fold_in(rng, 6)
    for dim, shards_of in split:
        steps = jnp.exp(jax.random.uniform(jax.random.fold_in(own, dim), (shards_of,), jnp.float32, low / len(split), top_value / len(split)))
        gain = gain * jnp.repeat(steps, shape[dim] // shards_of).reshape([-1 if axis == dim else 1 for axis in range(len(shape))])
    return gain


def centred(stream_key, shape, spread, reach, split=(), kind=jnp.bfloat16):
    gain = levels(stream_key, shape, split, -0.22, 0.18) if split else 1.0
    result = jax.random.normal(stream_key, shape, jnp.float32) * spread * gain
    return jnp.minimum(jnp.maximum(result, -reach), reach).astype(kind)


def setup_inputs(seed: int = 0) -> dict:
    keys = jax.random.split(jax.random.key(seed), 6)
    return {
        "adjoint_final": centred(keys[0], (SOLUTES, NX, NY, NZ), 1.0, 6.0, ((1, 16), (2, 8), (3, 4)), jnp.float32),
        "velocity": centred(keys[1], (3, NX, NY, NZ), 0.06, 0.15, ((1, 512),), jnp.float32),
        "diffusivity": jnp.clip(jnp.exp(math.log(0.04) - 1.3862944 * jax.random.uniform(keys[2], (SOLUTES, NX, NY, NZ), jnp.float32) ** levels(keys[2], (SOLUTES, NX, NY, NZ), ((1, 16), (2, 8), (3, 4)), -0.2, 0.2)), 0.01, 0.04),
        "upwind_side": with_ends((jax.random.randint(keys[3], (3, NX, NY, NZ), 0, 2) < 1).astype(jnp.int32), jax.random.fold_in(keys[3], 1), 0, 1),
        "wall_mask": with_ends((jax.random.randint(keys[4], (NX, NY, NZ), 0, 8) < 1).astype(jnp.int32), jax.random.fold_in(keys[4], 1), 0, 1),
    }


step_scale = 0.8
half_scale = 0.4


def shift_upper(field, dim):
    extent = field.shape[dim]
    inner = lax.slice_in_dim(field, 1, extent, axis=dim)
    zeros = jnp.zeros_like(lax.slice_in_dim(field, 0, 1, axis=dim))
    return jnp.concatenate([inner, zeros], axis=dim)


def shift_lower(field, dim):
    extent = field.shape[dim]
    inner = lax.slice_in_dim(field, 0, extent - 1, axis=dim)
    zeros = jnp.zeros_like(lax.slice_in_dim(field, 0, 1, axis=dim))
    return jnp.concatenate([zeros, inner], axis=dim)


def face_terms(which, forward, backward, diffusivity):
    extent = diffusivity.shape[which + 1]
    shape = [1, 1, 1, 1]
    shape[which + 1] = extent
    place = jnp.arange(extent, dtype=jnp.int32).reshape(shape)
    valid_up = (place < extent - 1).astype(jnp.float32)
    valid_dn = (place > 0).astype(jnp.float32)
    upper = valid_up * (forward[which:which + 1] + half_scale * (diffusivity + shift_upper(diffusivity, which + 1)))
    lower = valid_dn * (shift_lower(backward[which:which + 1], which + 1) + half_scale * (shift_lower(diffusivity, which + 1) + diffusivity))
    return upper, lower


def reference(adjoint_final, velocity, diffusivity, upwind_side, wall_mask):
    speed = jnp.abs(velocity)
    side = upwind_side.astype(jnp.float32)
    forward = step_scale * speed * side
    backward = step_scale * speed * (1.0 - side)
    keep = (1 - wall_mask).astype(jnp.float32)[None]
    adjoint = adjoint_final
    for step in range(STEPS):
        change = jnp.zeros_like(adjoint)
        for which in range(3):
            upper, lower = face_terms(which, forward, backward, diffusivity)
            above = shift_upper(adjoint, which + 1)
            below = shift_lower(adjoint, which + 1)
            change = change + upper * (above - adjoint) + lower * (below - adjoint)
        adjoint = keep * (adjoint + change)
    return adjoint
```

```python
import functools

import jax
import jax.numpy as jnp
from jax import lax
from jax.experimental import pallas as pl
from jax.experimental.pallas import tpu as pltpu
from jax.sharding import PartitionSpec as P

MESH = pl.DeviceIdType.MESH
STEPS = 5
AXES = ("gx", "gy", "gz")
DIF, BACK = STEPS + 1, STEPS + 2

step_scale = 0.8
half_scale = 0.4


def kernel(
    dims, counts,
    adj_h, vel_h, dif_h, side_h, wall_h, out_h,
    A, V, D, S, W, B, C, K, ysnd, yrcv, zsnd, zrcv,
    load_sem, vsend, vrecv, fsend, frecv, out_sem,
):
    SOL, NXL, NYL, NZL = dims
    ny, nz = counts[1], counts[2]
    group = ny * nz
    place = [lax.axis_index(a) for a in AXES]
    has_up = [place[i] < counts[i] - 1 for i in range(3)]
    has_dn = [place[i] > 0 for i in range(3)]
    me = place[1] * nz + place[2]

    loads = [
        pltpu.make_async_copy(adj_h, A.at[0, :, pl.ds(1, NXL)], load_sem.at[0]),
        pltpu.make_async_copy(dif_h, D.at[:, pl.ds(1, NXL)], load_sem.at[1]),
        pltpu.make_async_copy(side_h, S, load_sem.at[2]),
        pltpu.make_async_copy(wall_h, W, load_sem.at[3]),
    ]
    for c in loads:
        c.start()

    barrier = pltpu.get_barrier_semaphore()

    def peer(o):
        p = lax.rem(me + o, group)
        return p // nz, lax.rem(p, nz), p

    @pl.loop(1, group)
    def _(o):
        py, pz, _ = peer(o)
        pl.semaphore_signal(barrier, 1, device_id={"gy": py, "gz": pz}, device_id_type=MESH)

    for cond, d in ((has_up[0], 1), (has_dn[0], -1)):
        @pl.when(cond)
        def _():
            pl.semaphore_signal(barrier, 1, device_id={"gx": place[0] + d}, device_id_type=MESH)

    def face(m, dim, side):
        send, recv = fsend.at[m, dim, side], frecv.at[m, dim, side]
        to = {AXES[dim]: place[dim] + (1 - 2 * side)}
        if dim == 0:
            src_plane, dst_plane = (NXL, 0) if side == 0 else (1, NXL + 1)
            if isinstance(m, int) and m == BACK:
                src, dst = B.at[pl.ds(NXL, 1)], B.at[pl.ds(0, 1)]
            elif isinstance(m, int) and m == DIF:
                src, dst = D.at[:, pl.ds(src_plane, 1)], D.at[:, pl.ds(dst_plane, 1)]
            else:
                src, dst = A.at[m, :, pl.ds(src_plane, 1)], A.at[m, :, pl.ds(dst_plane, 1)]
        elif dim == 1:
            if isinstance(m, int) and m == BACK:
                src, dst = ysnd.at[m, side, pl.ds(0, NXL)], yrcv.at[m, side, pl.ds(0, NXL)]
            else:
                src, dst = ysnd.at[m, side], yrcv.at[m, side]
        else:
            src, dst = zsnd.at[m, side], zrcv.at[m, side]
        return pltpu.make_async_remote_copy(
            src_ref=src, dst_ref=dst, send_sem=send, recv_sem=recv, device_id=to, device_id_type=MESH
        )

    def sides(dim):
        return ((0, has_up[dim], has_dn[dim]), (1, has_dn[dim], has_up[dim]))

    def send_face(m, dim, only=None):
        for side, to, _ in sides(dim):
            if only is None or side == only:
                @pl.when(to)
                def _():
                    face(m, dim, side).start()

    def wait_face(m, dim, only=None):
        for side, _, fro in sides(dim):
            if only is None or side == only:
                @pl.when(fro)
                def _():
                    face(m, dim, side).wait_recv()

    def sent_face(m, dim, only=None):
        for side, to, _ in sides(dim):
            if only is None or side == only:
                @pl.when(to)
                def _():
                    face(m, dim, side).wait_send()

    for dim in range(3):
        for side, _, fro in sides(dim):
            @pl.when(jnp.logical_not(fro))
            def _():
                if dim == 0:
                    p = 0 if side == 0 else NXL + 1
                    for t in range(STEPS):
                        A[t, :, p] = jnp.zeros((SOL, NYL, NZL), jnp.float32)
                    D[:, p] = jnp.zeros((SOL, NYL, NZL), jnp.float32)
                    if side == 0:
                        B[0] = jnp.zeros((NYL, NZL), jnp.float32)
                elif dim == 1:
                    for m in range(STEPS + 3):
                        yrcv[m, side] = jnp.zeros(yrcv.shape[2:], jnp.float32)
                else:
                    for m in range(STEPS + 3):
                        zrcv[m, side] = jnp.zeros(zrcv.shape[2:], jnp.float32)

    lane = lax.broadcasted_iota(jnp.int32, (NYL, NZL), 1)
    row = lax.broadcasted_iota(jnp.int32, (NYL, NZL), 0)
    first_row, last_row = row == 0, row == NYL - 1
    first_lane, last_lane = lane == 0, lane == NZL - 1

    def pack(packs, v, k):
        r = pltpu.roll(v, (k + 1) % NZL, 1)
        return jnp.where(lane == k, r, packs[0]), jnp.where(lane == k + 1, r, packs[1])

    def no_packs():
        return jnp.zeros((NYL, NZL), jnp.float32), jnp.zeros((NYL, NZL), jnp.float32)

    def y_pair(v, m, k):
        up = jnp.where(last_row, yrcv[m, 1, pl.ds(k, 1), :], pltpu.roll(v, NYL - 1, 0))
        dn = jnp.where(first_row, yrcv[m, 0, pl.ds(k, 1), :], pltpu.roll(v, 1, 0))
        return up, dn

    def z_pair(v, zr, k):
        up = jnp.where(last_lane, pltpu.roll(zr[1], (NZL - 2 - k) % NZL, 1), pltpu.roll(v, NZL - 1, 1))
        dn = jnp.where(first_lane, pltpu.roll(zr[0], (NZL - k) % NZL, 1), pltpu.roll(v, 1, 1))
        return up, dn

    for c in loads[:2]:
        c.wait()
    for m, src in ((0, A.at[0]), (DIF, D)):
        packs = no_packs()
        for s in range(SOL):
            for x in range(NXL):
                k = s * NXL + x
                v = src[s, x + 1]
                ysnd[m, 0, pl.ds(k, 1), :] = v[NYL - 1:, :]
                ysnd[m, 1, pl.ds(k, 1), :] = v[:1, :]
                packs = pack(packs, v, k)
        zsnd[m, 0], zsnd[m, 1] = packs

    pl.semaphore_wait(
        barrier, group - 1 + has_up[0].astype(jnp.int32) + has_dn[0].astype(jnp.int32)
    )

    def block(p, py, pz, slot):
        return pltpu.make_async_remote_copy(
            src_ref=vel_h.at[:, 0, pl.ds(pl.multiple_of(py * NYL, NYL), NYL), pl.ds(pl.multiple_of(pz * NZL, NZL), NZL)],
            dst_ref=V.at[:, slot],
            send_sem=vsend.at[p],
            recv_sem=vrecv.at[slot],
            device_id={"gy": py, "gz": pz},
            device_id_type=MESH,
        )

    @pl.loop(1, group)
    def _(o):
        py, pz, p = peer(o)
        block(p, py, pz, me).start()

    own = pltpu.make_async_copy(
        vel_h.at[:, 0, pl.ds(pl.multiple_of(place[1] * NYL, NYL), NYL), pl.ds(pl.multiple_of(place[2] * NZL, NZL), NZL)],
        V.at[:, me],
        vrecv.at[me],
    )
    own.start()
    for m in (0, DIF):
        for dim in range(3):
            send_face(m, dim)

    for c in loads[2:]:
        c.wait()
    own.wait()

    @pl.loop(1, group)
    def _(o):
        py, pz, p = peer(o)
        block(p, py, pz, p).wait_recv()

    def backward(c, x):
        v = step_scale * jnp.abs(V[c, x])
        return v * (1.0 - S[c, x].astype(jnp.float32))

    for x in reversed(range(NXL)):
        B[x + 1] = backward(0, x)
        if x == NXL - 1:
            send_face(BACK, 0, 0)
    zp = no_packs()
    for x in range(NXL):
        ysnd[BACK, 0, pl.ds(x, 1), :] = backward(1, x)[NYL - 1:, :]
        zp = pack(zp, backward(2, x), x)
    zsnd[BACK, 0] = zp[0]
    send_face(BACK, 1, 0)
    send_face(BACK, 2, 0)

    for dim in range(3):
        wait_face(DIF, dim)
    for dim in range(3):
        wait_face(BACK, dim, 0)

    up_y = jnp.logical_or(jnp.logical_not(last_row), has_up[1]).astype(jnp.float32)
    dn_y = jnp.logical_or(jnp.logical_not(first_row), has_dn[1]).astype(jnp.float32)
    up_z = jnp.logical_or(jnp.logical_not(last_lane), has_up[2]).astype(jnp.float32)
    dn_z = jnp.logical_or(jnp.logical_not(first_lane), has_dn[2]).astype(jnp.float32)
    up_x = jnp.where(has_up[0], 1.0, 0.0).astype(jnp.float32)
    dn_x = jnp.where(has_dn[0], 1.0, 0.0).astype(jnp.float32)

    zd = (zrcv[DIF, 0], zrcv[DIF, 1])
    zb = zrcv[BACK, 0]
    for x in range(NXL):
        keep = (1 - W[x]).astype(jnp.float32)
        forward, back = [], []
        for c in range(3):
            v = step_scale * jnp.abs(V[c, x])
            side = S[c, x].astype(jnp.float32)
            forward.append(v * side)
            back.append(v * (1.0 - side))
        below_x = B[x]
        below_y = jnp.where(first_row, yrcv[BACK, 0, pl.ds(x, 1), :], pltpu.roll(back[1], 1, 0))
        below_z = jnp.where(first_lane, pltpu.roll(zb, (NZL - x) % NZL, 1), pltpu.roll(back[2], 1, 1))
        for s in range(SOL):
            k = s * NXL + x
            d = D[s, x + 1]
            yu, yl = y_pair(d, DIF, k)
            zu, zl = z_pair(d, zd, k)
            c0 = forward[0] + half_scale * (d + D[s, x + 2])
            c1 = below_x + half_scale * (d + D[s, x])
            if x == NXL - 1:
                c0 = c0 * up_x
            if x == 0:
                c1 = c1 * dn_x
            c2 = up_y * (forward[1] + half_scale * (d + yu))
            c3 = dn_y * (below_y + half_scale * (d + yl))
            c4 = up_z * (forward[2] + half_scale * (d + zu))
            c5 = dn_z * (below_z + half_scale * (d + zl))
            K[s, x] = keep * (1.0 - (((c0 + c1) + (c2 + c3)) + (c4 + c5)))
            for i, c in enumerate((c0, c1, c2, c3, c4, c5)):
                C[i, s, x] = keep * c

    order = [0, NXL - 1] + list(range(1, NXL - 1))

    @pl.loop(0, STEPS)
    def _(t):
        for dim in range(3):
            wait_face(t, dim)
        zr = (zrcv[t, 0], zrcv[t, 1])
        packs = no_packs()
        for i, x in enumerate(order):
            for s in range(SOL):
                k = s * NXL + x
                a = A[t, s, x + 1]
                yu, yl = y_pair(a, t, k)
                zu, zl = z_pair(a, zr, k)
                new = (
                    (K[s, x] * a + C[0, s, x] * A[t, s, x + 2] + C[1, s, x] * A[t, s, x])
                    + (C[2, s, x] * yu + C[3, s, x] * yl)
                    + (C[4, s, x] * zu + C[5, s, x] * zl)
                )
                A[t + 1, s, x + 1] = new
                ysnd[t + 1, 0, pl.ds(k, 1), :] = new[NYL - 1:, :]
                ysnd[t + 1, 1, pl.ds(k, 1), :] = new[:1, :]
                packs = pack(packs, new, k)
            if i == 1:
                @pl.when(t < STEPS - 1)
                def _():
                    send_face(t + 1, 0)
        zsnd[t + 1, 0], zsnd[t + 1, 1] = packs

        @pl.when(t < STEPS - 1)
        def _():
            send_face(t + 1, 1)
            send_face(t + 1, 2)

    out = pltpu.make_async_copy(A.at[STEPS, :, pl.ds(1, NXL)], out_h, out_sem)
    out.start()
    for m in range(STEPS):
        for dim in range(3):
            sent_face(m, dim)
    for dim in range(3):
        sent_face(DIF, dim)
        sent_face(BACK, dim, 0)

    @pl.loop(1, group)
    def _(o):
        py, pz, p = peer(o)
        block(p, py, pz, me).wait_send()

    out.wait()


def solution(mesh):
    counts = tuple(mesh.shape[a] for a in AXES)

    def local(adjoint_final, velocity, diffusivity, upwind_side, wall_mask):
        dims = adjoint_final.shape
        sol, nxl, nyl, nzl = dims
        f32 = jnp.float32
        group = counts[1] * counts[2]
        messages = STEPS + 3
        return pl.pallas_call(
            functools.partial(kernel, dims, counts),
            out_shape=jax.ShapeDtypeStruct(dims, f32),
            in_specs=[pl.BlockSpec(memory_space=pl.ANY)] * 5,
            out_specs=pl.BlockSpec(memory_space=pl.ANY),
            scratch_shapes=[
                pltpu.VMEM((STEPS + 1, sol, nxl + 2, nyl, nzl), f32),
                pltpu.VMEM((3, nxl, nyl, nzl), f32),
                pltpu.VMEM((sol, nxl + 2, nyl, nzl), f32),
                pltpu.VMEM((3, nxl, nyl, nzl), jnp.int32),
                pltpu.VMEM((nxl, nyl, nzl), jnp.int32),
                pltpu.VMEM((nxl + 1, nyl, nzl), f32),
                pltpu.VMEM((6, sol, nxl, nyl, nzl), f32),
                pltpu.VMEM((sol, nxl, nyl, nzl), f32),
                pltpu.VMEM((messages, 2, sol * nxl, nzl), f32),
                pltpu.VMEM((messages, 2, sol * nxl, nzl), f32),
                pltpu.VMEM((messages, 2, nyl, nzl), f32),
                pltpu.VMEM((messages, 2, nyl, nzl), f32),
                pltpu.SemaphoreType.DMA((4,)),
                pltpu.SemaphoreType.DMA((group,)),
                pltpu.SemaphoreType.DMA((group,)),
                pltpu.SemaphoreType.DMA((messages, 3, 2)),
                pltpu.SemaphoreType.DMA((messages, 3, 2)),
                pltpu.SemaphoreType.DMA,
            ],
            compiler_params=pltpu.CompilerParams(
                collective_id=0, has_side_effects=True, vmem_limit_bytes=48 << 20
            ),
        )(adjoint_final, velocity, diffusivity, upwind_side, wall_mask)

    return jax.shard_map(
        local,
        mesh=mesh,
        in_specs=(
            P(None, "gx", "gy", "gz"),
            P(None, ("gx", "gy", "gz"), None, None),
            P(None, "gx", "gy", "gz"),
            P(None, "gx", "gy", "gz"),
            P("gx", "gy", "gz"),
        ),
        out_specs=P(None, "gx", "gy", "gz"),
        check_vma=False,
    )
```

```python
import functools

import jax
import jax.numpy as jnp
from jax import lax
from jax.experimental import pallas as pl
from jax.experimental.pallas import tpu as pltpu
from jax.sharding import PartitionSpec as P

MESH = pl.DeviceIdType.MESH
STEPS = 5
AXES = ("gx", "gy", "gz")
DIF, BACK, COEF = STEPS + 1, STEPS + 2, STEPS + 3

step_scale = 0.8
half_scale = 0.4


def kernel(
    dims, counts,
    adj_h, vel_h, dif_h, side_h, wall_h, out_h,
    A, V, D, S, W, B, C, K, ysnd, yrcv, zsnd, zrcv, late, edge_v,
    load_sem, vsend, vrecv, esend, erecv, fsend, frecv, out_sem,
):
    SOL, NXL, NYL, NZL = dims
    ny, nz = counts[1], counts[2]
    group = ny * nz
    place = [lax.axis_index(a) for a in AXES]
    has_up = [place[i] < counts[i] - 1 for i in range(3)]
    has_dn = [place[i] > 0 for i in range(3)]
    me = place[1] * nz + place[2]
    half = ny // 2
    far = (place[1] == half - 1, place[1] == half)
    near_dn = jnp.logical_and(has_dn[1], jnp.logical_not(far[1]))
    near_up = jnp.logical_and(has_up[1], jnp.logical_not(far[0]))

    loads = [
        pltpu.make_async_copy(adj_h, A.at[0, :, pl.ds(1, NXL)], load_sem.at[0]),
        pltpu.make_async_copy(dif_h, D.at[:, pl.ds(1, NXL)], load_sem.at[1]),
        pltpu.make_async_copy(side_h, S, load_sem.at[2]),
        pltpu.make_async_copy(wall_h, W, load_sem.at[3]),
    ]
    for c in loads:
        c.start()

    barrier = pltpu.get_barrier_semaphore()

    def peer(o):
        p = lax.rem(me + o, group)
        return p // nz, lax.rem(p, nz), p

    @pl.loop(1, group)
    def _(o):
        py, pz, _ = peer(o)
        pl.semaphore_signal(barrier, 1, device_id={"gy": py, "gz": pz}, device_id_type=MESH)

    for cond, d in ((has_up[0], 1), (has_dn[0], -1)):
        @pl.when(cond)
        def _():
            pl.semaphore_signal(barrier, 1, device_id={"gx": place[0] + d}, device_id_type=MESH)

    def face(m, dim, side):
        send, recv = fsend.at[m, dim, side], frecv.at[m, dim, side]
        to = {AXES[dim]: place[dim] + (1 - 2 * side)}
        if dim == 0:
            src_plane, dst_plane = (NXL, 0) if side == 0 else (1, NXL + 1)
            if m == BACK:
                src, dst = B.at[pl.ds(NXL, 1)], B.at[pl.ds(0, 1)]
            elif m == DIF:
                src, dst = D.at[:, pl.ds(src_plane, 1)], D.at[:, pl.ds(dst_plane, 1)]
            else:
                src, dst = A.at[m, :, pl.ds(src_plane, 1)], A.at[m, :, pl.ds(dst_plane, 1)]
        elif dim == 1:
            if m == BACK:
                src, dst = ysnd.at[m, side, pl.ds(0, NXL)], yrcv.at[m, side, pl.ds(0, NXL)]
            else:
                src, dst = ysnd.at[m, side], yrcv.at[m, side]
        else:
            src, dst = zsnd.at[m, side], zrcv.at[m, side]
        return pltpu.make_async_remote_copy(
            src_ref=src, dst_ref=dst, send_sem=send, recv_sem=recv, device_id=to, device_id_type=MESH
        )

    def far_face(m, side):
        src, dst = ysnd.at[m, side], late.at[m // 2] if m < STEPS and m % 2 else yrcv.at[m, side]
        if m == BACK:
            src, dst = src.at[pl.ds(0, NXL)], dst.at[pl.ds(0, NXL)]
        return pltpu.make_async_remote_copy(
            src_ref=src, dst_ref=dst, send_sem=fsend.at[m, 1, side], recv_sem=frecv.at[m, 1, side],
            device_id={"gy": place[1] + (1 - 2 * side)}, device_id_type=MESH,
        )

    def both_far(act):
        for side in (0, 1):
            @pl.when(far[side])
            def _():
                act(side)

    def sides(dim):
        if dim == 1:
            return ((0, near_up, near_dn), (1, near_dn, near_up))
        return ((0, has_up[dim], has_dn[dim]), (1, has_dn[dim], has_up[dim]))

    def send_face(m, dim, only=None):
        for side, to, _ in sides(dim):
            if only is None or side == only:
                @pl.when(to)
                def _():
                    face(m, dim, side).start()

    def wait_face(m, dim, only=None):
        for side, _, fro in sides(dim):
            if only is None or side == only:
                @pl.when(fro)
                def _():
                    face(m, dim, side).wait_recv()

    def sent_face(m, dim, only=None):
        for side, to, _ in sides(dim):
            if only is None or side == only:
                @pl.when(to)
                def _():
                    face(m, dim, side).wait_send()

    for dim in range(3):
        for side, _, fro in sides(dim):
            outside = jnp.logical_not((has_dn, has_up)[side][dim])

            @pl.when(outside)
            def _():
                if dim == 0:
                    p = 0 if side == 0 else NXL + 1
                    for t in range(STEPS):
                        A[t, :, p] = jnp.zeros((SOL, NYL, NZL), jnp.float32)
                    D[:, p] = jnp.zeros((SOL, NYL, NZL), jnp.float32)
                    if side == 0:
                        B[0] = jnp.zeros((NYL, NZL), jnp.float32)
                elif dim == 1:
                    for m in range(STEPS + 4):
                        yrcv[m, side] = jnp.zeros(yrcv.shape[2:], jnp.float32)
                else:
                    for m in range(STEPS + 4):
                        zrcv[m, side] = jnp.zeros(zrcv.shape[2:], jnp.float32)

    def clear_late(side):
        for m in range(1, STEPS, 2):
            yrcv[m, 1 - side] = jnp.zeros(yrcv.shape[2:], jnp.float32)

    both_far(clear_late)

    lane = lax.broadcasted_iota(jnp.int32, (NYL, NZL), 1)
    row = lax.broadcasted_iota(jnp.int32, (NYL, NZL), 0)
    first_row, last_row = row == 0, row == NYL - 1
    first_lane, last_lane = lane == 0, lane == NZL - 1

    def pack(packs, v, k):
        r = pltpu.roll(v, (k + 1) % NZL, 1)
        return jnp.where(lane == k, r, packs[0]), jnp.where(lane == k + 1, r, packs[1])

    def no_packs():
        return jnp.zeros((NYL, NZL), jnp.float32), jnp.zeros((NYL, NZL), jnp.float32)

    def y_pair(v, m, k):
        up = jnp.where(last_row, yrcv[m, 1, pl.ds(k, 1), :], pltpu.roll(v, NYL - 1, 0))
        dn = jnp.where(first_row, yrcv[m, 0, pl.ds(k, 1), :], pltpu.roll(v, 1, 0))
        return up, dn

    def z_pair(v, zr, k):
        up = jnp.where(last_lane, pltpu.roll(zr[1], (NZL - 2 - k) % NZL, 1), pltpu.roll(v, NZL - 1, 1))
        dn = jnp.where(first_lane, pltpu.roll(zr[0], (NZL - k) % NZL, 1), pltpu.roll(v, 1, 1))
        return up, dn

    for c in loads[:2]:
        c.wait()
    for m, src in ((0, A.at[0]), (DIF, D)):
        packs = no_packs()
        for s in range(SOL):
            for x in range(NXL):
                k = s * NXL + x
                v = src[s, x + 1]
                ysnd[m, 0, pl.ds(k, 1), :] = v[NYL - 1:, :]
                ysnd[m, 1, pl.ds(k, 1), :] = v[:1, :]
                packs = pack(packs, v, k)
        zsnd[m, 0], zsnd[m, 1] = packs

    pl.semaphore_wait(
        barrier, group - 1 + has_up[0].astype(jnp.int32) + has_dn[0].astype(jnp.int32)
    )

    def block(p, py, pz, slot):
        return pltpu.make_async_remote_copy(
            src_ref=vel_h.at[:, 0, pl.ds(pl.multiple_of(py * NYL, NYL), NYL), pl.ds(pl.multiple_of(pz * NZL, NZL), NZL)],
            dst_ref=V.at[:, slot],
            send_sem=vsend.at[p],
            recv_sem=vrecv.at[slot],
            device_id={"gy": py, "gz": pz},
            device_id_type=MESH,
        )

    def edge(p, pz, slot):
        return pltpu.make_async_remote_copy(
            src_ref=vel_h.at[1, 0, pl.ds((half - 1) * NYL, NYL), pl.ds(pl.multiple_of(pz * NZL, NZL), NZL)],
            dst_ref=edge_v.at[slot],
            send_sem=esend.at[p],
            recv_sem=erecv.at[slot],
            device_id={"gy": half, "gz": pz},
            device_id_type=MESH,
        )

    @pl.loop(1, group)
    def _(o):
        py, pz, p = peer(o)
        block(p, py, pz, me).start()

        @pl.when(py == half)
        def _():
            edge(p, pz, me).start()

    own_edge = pltpu.make_async_copy(
        vel_h.at[1, 0, pl.ds((half - 1) * NYL, NYL), pl.ds(pl.multiple_of(place[2] * NZL, NZL), NZL)],
        edge_v.at[me],
        erecv.at[me],
    )

    @pl.when(far[1])
    def _():
        own_edge.start()

    own = pltpu.make_async_copy(
        vel_h.at[:, 0, pl.ds(pl.multiple_of(place[1] * NYL, NYL), NYL), pl.ds(pl.multiple_of(place[2] * NZL, NZL), NZL)],
        V.at[:, me],
        vrecv.at[me],
    )
    own.start()
    for m in (0, DIF):
        for dim in range(3):
            send_face(m, dim)
        both_far(lambda side: far_face(m, side).start())

    for c in loads[2:]:
        c.wait()

    @pl.when(far[0])
    def _():
        for x in range(NXL):
            ysnd[BACK, 0, pl.ds(x, 1), :] = step_scale * (1.0 - S[1, x][NYL - 1:, :].astype(jnp.float32))
        far_face(BACK, 0).start()

    own.wait()

    @pl.when(far[1])
    def _():
        own_edge.wait()

        @pl.loop(1, group)
        def _(o):
            py, pz, p = peer(o)
            edge(p, pz, p).wait_recv()

    @pl.loop(1, group)
    def _(o):
        py, pz, p = peer(o)
        block(p, py, pz, p).wait_recv()

    def backward(c, x):
        v = step_scale * jnp.abs(V[c, x])
        return v * (1.0 - S[c, x].astype(jnp.float32))

    for x in reversed(range(NXL)):
        B[x + 1] = backward(0, x)
        if x == NXL - 1:
            send_face(BACK, 0, 0)
    zp = no_packs()
    for x in range(NXL):
        zp = pack(zp, backward(2, x), x)
    zsnd[BACK, 0] = zp[0]
    send_face(BACK, 2, 0)

    @pl.when(near_up)
    def _():
        for x in range(NXL):
            ysnd[BACK, 0, pl.ds(x, 1), :] = backward(1, x)[NYL - 1:, :]

    send_face(BACK, 1, 0)

    for dim in range(3):
        wait_face(DIF, dim)
    both_far(lambda side: far_face(DIF, 1 - side).wait_recv())
    for dim in range(3):
        wait_face(BACK, dim, 0)

    @pl.when(far[1])
    def _():
        far_face(BACK, 0).wait_recv()
        for x in range(NXL):
            yrcv[BACK, 0, pl.ds(x, 1), :] = yrcv[BACK, 0, pl.ds(x, 1), :] * jnp.abs(edge_v[x][NYL - 1:, :])

    up_y = jnp.logical_or(jnp.logical_not(last_row), has_up[1]).astype(jnp.float32)
    dn_y = jnp.logical_or(jnp.logical_not(first_row), has_dn[1]).astype(jnp.float32)
    up_z = jnp.logical_or(jnp.logical_not(last_lane), has_up[2]).astype(jnp.float32)
    dn_z = jnp.logical_or(jnp.logical_not(first_lane), has_dn[2]).astype(jnp.float32)
    up_x = jnp.where(has_up[0], 1.0, 0.0).astype(jnp.float32)
    dn_x = jnp.where(has_dn[0], 1.0, 0.0).astype(jnp.float32)

    zd = (zrcv[DIF, 0], zrcv[DIF, 1])
    zb = zrcv[BACK, 0]
    for x in range(NXL):
        keep = (1 - W[x]).astype(jnp.float32)
        forward, back = [], []
        for c in range(3):
            v = step_scale * jnp.abs(V[c, x])
            side = S[c, x].astype(jnp.float32)
            forward.append(v * side)
            back.append(v * (1.0 - side))
        below_x = B[x]
        below_y = jnp.where(first_row, yrcv[BACK, 0, pl.ds(x, 1), :], pltpu.roll(back[1], 1, 0))
        below_z = jnp.where(first_lane, pltpu.roll(zb, (NZL - x) % NZL, 1), pltpu.roll(back[2], 1, 1))
        for s in range(SOL):
            k = s * NXL + x
            d = D[s, x + 1]
            yu, yl = y_pair(d, DIF, k)
            zu, zl = z_pair(d, zd, k)
            c0 = forward[0] + half_scale * (d + D[s, x + 2])
            c1 = below_x + half_scale * (d + D[s, x])
            if x == NXL - 1:
                c0 = c0 * up_x
            if x == 0:
                c1 = c1 * dn_x
            c2 = up_y * (forward[1] + half_scale * (d + yu))
            c3 = dn_y * (below_y + half_scale * (d + yl))
            c4 = up_z * (forward[2] + half_scale * (d + zu))
            c5 = dn_z * (below_z + half_scale * (d + zl))
            K[s, x] = keep * (1.0 - (((c0 + c1) + (c2 + c3)) + (c4 + c5)))
            for i, c in enumerate((c0, c1, c2, c3, c4, c5)):
                C[i, s, x] = keep * c

    def send_coef(side):
        for k in range(SOL * NXL):
            c = C[2 + side, k // NXL, k % NXL]
            ysnd[COEF, side, pl.ds(k, 1), :] = c[NYL - 1:, :] if side == 0 else c[:1, :]
        far_face(COEF, side).start()

    both_far(send_coef)

    for t in range(STEPS):
        for dim in range(3):
            wait_face(t, dim)

        if t % 2 == 0:
            def arrived(side):
                far_face(t, 1 - side).wait_recv()
                if t == 2:
                    far_face(COEF, 1 - side).wait_recv()
                if t > 0:
                    yrcv[t, 1 - side] = yrcv[t, 1 - side] + yrcv[COEF, 1 - side] * ysnd[t - 1, side]

            both_far(arrived)

        zr = (zrcv[t, 0], zrcv[t, 1])
        for x in range(NXL):
            for s in range(SOL):
                k = s * NXL + x
                a = A[t, s, x + 1]
                yu, yl = y_pair(a, t, k)
                zu, zl = z_pair(a, zr, k)
                new = (
                    (K[s, x] * a + C[0, s, x] * A[t, s, x + 2] + C[1, s, x] * A[t, s, x])
                    + (C[2, s, x] * yu + C[3, s, x] * yl)
                    + (C[4, s, x] * zu + C[5, s, x] * zl)
                )
                A[t + 1, s, x + 1] = new
                ysnd[t + 1, 0, pl.ds(k, 1), :] = new[NYL - 1:, :]
                ysnd[t + 1, 1, pl.ds(k, 1), :] = new[:1, :]

        if t % 2:
            def finish(side):
                if t < STEPS - 1:
                    far_face(t + 1, side).start()
                far_face(t, 1 - side).wait_recv()
                rows = ysnd[t + 1, side] + ysnd[COEF, side] * late[t // 2]
                r = NYL - 1 if side == 0 else 0
                for k in range(SOL * NXL):
                    A[t + 1, k // NXL, k % NXL + 1, pl.ds(r, 1), :] = rows[k:k + 1, :]

            both_far(finish)

        if t < STEPS - 1:
            send_face(t + 1, 0)
            send_face(t + 1, 1)
            if t % 2 == 0:
                both_far(lambda side: far_face(t + 1, side).start())
            packs = no_packs()
            for k in range(SOL * NXL):
                packs = pack(packs, A[t + 1, k // NXL, k % NXL + 1], k)
            zsnd[t + 1, 0], zsnd[t + 1, 1] = packs
            send_face(t + 1, 2)

    out = pltpu.make_async_copy(A.at[STEPS, :, pl.ds(1, NXL)], out_h, out_sem)
    out.start()
    for m in range(STEPS):
        for dim in range(3):
            sent_face(m, dim)
    for dim in range(3):
        sent_face(DIF, dim)
        sent_face(BACK, dim, 0)

    def sent_far(side):
        for m in list(range(STEPS)) + [DIF, COEF]:
            far_face(m, side).wait_send()
        if side == 0:
            far_face(BACK, side).wait_send()

    both_far(sent_far)

    @pl.loop(1, group)
    def _(o):
        py, pz, p = peer(o)
        block(p, py, pz, me).wait_send()

        @pl.when(py == half)
        def _():
            edge(p, pz, me).wait_send()

    out.wait()


def solution(mesh):
    counts = tuple(mesh.shape[a] for a in AXES)

    def local(adjoint_final, velocity, diffusivity, upwind_side, wall_mask):
        dims = adjoint_final.shape
        sol, nxl, nyl, nzl = dims
        f32 = jnp.float32
        group = counts[1] * counts[2]
        messages = STEPS + 4
        return pl.pallas_call(
            functools.partial(kernel, dims, counts),
            out_shape=jax.ShapeDtypeStruct(dims, f32),
            in_specs=[pl.BlockSpec(memory_space=pl.ANY)] * 5,
            out_specs=pl.BlockSpec(memory_space=pl.ANY),
            scratch_shapes=[
                pltpu.VMEM((STEPS + 1, sol, nxl + 2, nyl, nzl), f32),
                pltpu.VMEM((3, nxl, nyl, nzl), f32),
                pltpu.VMEM((sol, nxl + 2, nyl, nzl), f32),
                pltpu.VMEM((3, nxl, nyl, nzl), jnp.int32),
                pltpu.VMEM((nxl, nyl, nzl), jnp.int32),
                pltpu.VMEM((nxl + 1, nyl, nzl), f32),
                pltpu.VMEM((6, sol, nxl, nyl, nzl), f32),
                pltpu.VMEM((sol, nxl, nyl, nzl), f32),
                pltpu.VMEM((messages, 2, sol * nxl, nzl), f32),
                pltpu.VMEM((messages, 2, sol * nxl, nzl), f32),
                pltpu.VMEM((messages, 2, nyl, nzl), f32),
                pltpu.VMEM((messages, 2, nyl, nzl), f32),
                pltpu.VMEM((STEPS // 2, sol * nxl, nzl), f32),
                pltpu.VMEM((group, nyl, nzl), f32),
                pltpu.SemaphoreType.DMA((4,)),
                pltpu.SemaphoreType.DMA((group,)),
                pltpu.SemaphoreType.DMA((group,)),
                pltpu.SemaphoreType.DMA((group,)),
                pltpu.SemaphoreType.DMA((group,)),
                pltpu.SemaphoreType.DMA((messages, 3, 2)),
                pltpu.SemaphoreType.DMA((messages, 3, 2)),
                pltpu.SemaphoreType.DMA,
            ],
            compiler_params=pltpu.CompilerParams(
                collective_id=0, has_side_effects=True, vmem_limit_bytes=62 << 20
            ),
        )(adjoint_final, velocity, diffusivity, upwind_side, wall_mask)

    return jax.shard_map(
        local,
        mesh=mesh,
        in_specs=(
            P(None, "gx", "gy", "gz"),
            P(None, ("gx", "gy", "gz"), None, None),
            P(None, "gx", "gy", "gz"),
            P(None, "gx", "gy", "gz"),
            P("gx", "gy", "gz"),
        ),
        out_specs=P(None, "gx", "gy", "gz"),
        check_vma=False,
    )
```

```python
import functools

import jax
import jax.numpy as jnp
from jax import lax
from jax.experimental import pallas as pl
from jax.experimental.pallas import tpu as pltpu
from jax.sharding import PartitionSpec as P

MESH = pl.DeviceIdType.MESH
STEPS = 5
PARTS = 4
AXES = ("gx", "gy", "gz")
DIF, BACK, COEF = STEPS + 1, STEPS + 2, STEPS + 3

step_scale = 0.8
half_scale = 0.4


def kernel(
    dims, counts,
    adj_h, vel_h, dif_h, side_h, wall_h, out_h,
    A, V, D, S, W, B, C, K, ysnd, yrcv, zsnd, zrcv, late, edge_v,
    load_sem, vsend, vrecv, esend, erecv, fsend, frecv, out_sem,
):
    SOL, NXL, NYL, NZL = dims
    ny, nz = counts[1], counts[2]
    group = ny * nz
    place = [lax.axis_index(a) for a in AXES]
    has_up = [place[i] < counts[i] - 1 for i in range(3)]
    has_dn = [place[i] > 0 for i in range(3)]
    me = place[1] * nz + place[2]
    half = ny // 2
    far = (place[1] == half - 1, place[1] == half)
    near_dn = jnp.logical_and(has_dn[1], jnp.logical_not(far[1]))
    near_up = jnp.logical_and(has_up[1], jnp.logical_not(far[0]))

    loads = [
        pltpu.make_async_copy(adj_h, A.at[0, :, pl.ds(1, NXL)], load_sem.at[0]),
        pltpu.make_async_copy(dif_h, D.at[:, pl.ds(1, NXL)], load_sem.at[1]),
        pltpu.make_async_copy(side_h, S, load_sem.at[2]),
        pltpu.make_async_copy(wall_h, W, load_sem.at[3]),
    ]
    for c in loads:
        c.start()

    barrier = pltpu.get_barrier_semaphore()

    def peer(o):
        p = lax.rem(me + o, group)
        return p // nz, lax.rem(p, nz), p

    @pl.loop(1, group)
    def _(o):
        py, pz, _ = peer(o)
        pl.semaphore_signal(barrier, 1, device_id={"gy": py, "gz": pz}, device_id_type=MESH)

    for cond, d in ((has_up[0], 1), (has_dn[0], -1)):
        @pl.when(cond)
        def _():
            pl.semaphore_signal(barrier, 1, device_id={"gx": place[0] + d}, device_id_type=MESH)

    def face(m, dim, side):
        send, recv = fsend.at[m, dim, side], frecv.at[m, dim, side]
        to = {AXES[dim]: place[dim] + (1 - 2 * side)}
        if dim == 0:
            src_plane, dst_plane = (NXL, 0) if side == 0 else (1, NXL + 1)
            if m == BACK:
                src, dst = B.at[pl.ds(NXL, 1)], B.at[pl.ds(0, 1)]
            elif m == DIF:
                src, dst = D.at[:, pl.ds(src_plane, 1)], D.at[:, pl.ds(dst_plane, 1)]
            else:
                src, dst = A.at[m, :, pl.ds(src_plane, 1)], A.at[m, :, pl.ds(dst_plane, 1)]
        elif dim == 1:
            if m == BACK:
                src, dst = ysnd.at[m, side, pl.ds(0, NXL)], yrcv.at[m, side, pl.ds(0, NXL)]
            else:
                src, dst = ysnd.at[m, side], yrcv.at[m, side]
        else:
            src, dst = zsnd.at[m, side], zrcv.at[m, side]
        return pltpu.make_async_remote_copy(
            src_ref=src, dst_ref=dst, send_sem=send, recv_sem=recv, device_id=to, device_id_type=MESH
        )

    def far_face(m, side):
        src, dst = ysnd.at[m, side], late.at[m // 2] if m < STEPS and m % 2 else yrcv.at[m, side]
        if m == BACK:
            src, dst = src.at[pl.ds(0, NXL)], dst.at[pl.ds(0, NXL)]
        return pltpu.make_async_remote_copy(
            src_ref=src, dst_ref=dst, send_sem=fsend.at[m, 1, side], recv_sem=frecv.at[m, 1, side],
            device_id={"gy": place[1] + (1 - 2 * side)}, device_id_type=MESH,
        )

    def both_far(act):
        for side in (0, 1):
            @pl.when(far[side])
            def _():
                act(side)

    def sides(dim):
        if dim == 1:
            return ((0, near_up, near_dn), (1, near_dn, near_up))
        return ((0, has_up[dim], has_dn[dim]), (1, has_dn[dim], has_up[dim]))

    def send_face(m, dim, only=None):
        for side, to, _ in sides(dim):
            if only is None or side == only:
                @pl.when(to)
                def _():
                    face(m, dim, side).start()

    def wait_face(m, dim, only=None):
        for side, _, fro in sides(dim):
            if only is None or side == only:
                @pl.when(fro)
                def _():
                    face(m, dim, side).wait_recv()

    def sent_face(m, dim, only=None):
        for side, to, _ in sides(dim):
            if only is None or side == only:
                @pl.when(to)
                def _():
                    face(m, dim, side).wait_send()

    for dim in range(3):
        for side, _, fro in sides(dim):
            outside = jnp.logical_not((has_dn, has_up)[side][dim])

            @pl.when(outside)
            def _():
                if dim == 0:
                    p = 0 if side == 0 else NXL + 1
                    for t in range(STEPS):
                        A[t, :, p] = jnp.zeros((SOL, NYL, NZL), jnp.float32)
                    D[:, p] = jnp.zeros((SOL, NYL, NZL), jnp.float32)
                    if side == 0:
                        B[0] = jnp.zeros((NYL, NZL), jnp.float32)
                elif dim == 1:
                    for m in range(STEPS + 4):
                        yrcv[m, side] = jnp.zeros(yrcv.shape[2:], jnp.float32)
                else:
                    for m in range(STEPS + 4):
                        zrcv[m, side] = jnp.zeros(zrcv.shape[2:], jnp.float32)

    def clear_late(side):
        for m in range(1, STEPS, 2):
            yrcv[m, 1 - side] = jnp.zeros(yrcv.shape[2:], jnp.float32)

    both_far(clear_late)

    lane = lax.broadcasted_iota(jnp.int32, (NYL, NZL), 1)
    row = lax.broadcasted_iota(jnp.int32, (NYL, NZL), 0)
    first_row, last_row = row == 0, row == NYL - 1
    first_lane, last_lane = lane == 0, lane == NZL - 1

    def pack(packs, v, k):
        r = pltpu.roll(v, (k + 1) % NZL, 1)
        return jnp.where(lane == k, r, packs[0]), jnp.where(lane == k + 1, r, packs[1])

    def no_packs():
        return jnp.zeros((NYL, NZL), jnp.float32), jnp.zeros((NYL, NZL), jnp.float32)

    def y_pair(v, m, k):
        up = jnp.where(last_row, yrcv[m, 1, pl.ds(k, 1), :], pltpu.roll(v, NYL - 1, 0))
        dn = jnp.where(first_row, yrcv[m, 0, pl.ds(k, 1), :], pltpu.roll(v, 1, 0))
        return up, dn

    def z_pair(v, zr, k):
        up = jnp.where(last_lane, pltpu.roll(zr[1], (NZL - 2 - k) % NZL, 1), pltpu.roll(v, NZL - 1, 1))
        dn = jnp.where(first_lane, pltpu.roll(zr[0], (NZL - k) % NZL, 1), pltpu.roll(v, 1, 1))
        return up, dn

    for c in loads[:2]:
        c.wait()
    for m, src in ((0, A.at[0]), (DIF, D)):
        packs = no_packs()
        for s in range(SOL):
            for x in range(NXL):
                k = s * NXL + x
                v = src[s, x + 1]
                ysnd[m, 0, pl.ds(k, 1), :] = v[NYL - 1:, :]
                ysnd[m, 1, pl.ds(k, 1), :] = v[:1, :]
                packs = pack(packs, v, k)
        zsnd[m, 0], zsnd[m, 1] = packs

    pl.semaphore_wait(
        barrier, group - 1 + has_up[0].astype(jnp.int32) + has_dn[0].astype(jnp.int32)
    )

    def block(p, py, pz, slot):
        return pltpu.make_async_remote_copy(
            src_ref=vel_h.at[:, 0, pl.ds(pl.multiple_of(py * NYL, NYL), NYL), pl.ds(pl.multiple_of(pz * NZL, NZL), NZL)],
            dst_ref=V.at[:, slot],
            send_sem=vsend.at[p],
            recv_sem=vrecv.at[slot],
            device_id={"gy": py, "gz": pz},
            device_id_type=MESH,
        )

    def edge(p, pz, slot):
        return pltpu.make_async_remote_copy(
            src_ref=vel_h.at[1, 0, pl.ds((half - 1) * NYL, NYL), pl.ds(pl.multiple_of(pz * NZL, NZL), NZL)],
            dst_ref=edge_v.at[slot],
            send_sem=esend.at[p],
            recv_sem=erecv.at[slot],
            device_id={"gy": half, "gz": pz},
            device_id_type=MESH,
        )

    @pl.loop(1, group)
    def _(o):
        x, z = lax.rem(place[1], half), (place[1] // half) * nz + place[2]
        x, z = lax.rem(x + o // (2 * nz), half), lax.rem(z + o * 3, 2 * nz)
        py, pz = (z // nz) * half + x, lax.rem(z, nz)
        p = py * nz + pz
        block(p, py, pz, me).start()

        @pl.when(py == half)
        def _():
            edge(p, pz, me).start()

    own_edge = pltpu.make_async_copy(
        vel_h.at[1, 0, pl.ds((half - 1) * NYL, NYL), pl.ds(pl.multiple_of(place[2] * NZL, NZL), NZL)],
        edge_v.at[me],
        erecv.at[me],
    )

    @pl.when(far[1])
    def _():
        own_edge.start()

    own = pltpu.make_async_copy(
        vel_h.at[:, 0, pl.ds(pl.multiple_of(place[1] * NYL, NYL), NYL), pl.ds(pl.multiple_of(place[2] * NZL, NZL), NZL)],
        V.at[:, me],
        vrecv.at[me],
    )
    own.start()
    for m in (DIF, 0):
        both_far(lambda side: far_face(m, side).start())

    for c in loads[2:]:
        c.wait()

    @pl.when(far[0])
    def _():
        for x in range(NXL):
            ysnd[BACK, 0, pl.ds(x, 1), :] = step_scale * (1.0 - S[1, x][NYL - 1:, :].astype(jnp.float32))
        far_face(BACK, 0).start()

    for m in (DIF, 0):
        for dim in range(3):
            send_face(m, dim)

    own.wait()

    @pl.when(far[1])
    def _():
        own_edge.wait()

        @pl.loop(1, group)
        def _(o):
            py, pz, p = peer(o)
            edge(p, pz, p).wait_recv()

    @pl.loop(1, group)
    def _(o):
        py, pz, p = peer(o)
        block(p, py, pz, p).wait_recv()

    def backward(c, x):
        v = step_scale * jnp.abs(V[c, x])
        return v * (1.0 - S[c, x].astype(jnp.float32))

    for x in reversed(range(NXL)):
        B[x + 1] = backward(0, x)
        if x == NXL - 1:
            send_face(BACK, 0, 0)
    zp = no_packs()
    for x in range(NXL):
        zp = pack(zp, backward(2, x), x)
    zsnd[BACK, 0] = zp[0]
    send_face(BACK, 2, 0)

    @pl.when(near_up)
    def _():
        for x in range(NXL):
            ysnd[BACK, 0, pl.ds(x, 1), :] = backward(1, x)[NYL - 1:, :]

    send_face(BACK, 1, 0)

    for dim in range(3):
        wait_face(DIF, dim)
    both_far(lambda side: far_face(DIF, 1 - side).wait_recv())
    for dim in range(3):
        wait_face(BACK, dim, 0)

    @pl.when(far[1])
    def _():
        far_face(BACK, 0).wait_recv()
        for x in range(NXL):
            yrcv[BACK, 0, pl.ds(x, 1), :] = yrcv[BACK, 0, pl.ds(x, 1), :] * jnp.abs(edge_v[x][NYL - 1:, :])

    up_y = jnp.logical_or(jnp.logical_not(last_row), has_up[1]).astype(jnp.float32)
    dn_y = jnp.logical_or(jnp.logical_not(first_row), has_dn[1]).astype(jnp.float32)
    up_z = jnp.logical_or(jnp.logical_not(last_lane), has_up[2]).astype(jnp.float32)
    dn_z = jnp.logical_or(jnp.logical_not(first_lane), has_dn[2]).astype(jnp.float32)
    up_x = jnp.where(has_up[0], 1.0, 0.0).astype(jnp.float32)
    dn_x = jnp.where(has_dn[0], 1.0, 0.0).astype(jnp.float32)

    zd = (zrcv[DIF, 0], zrcv[DIF, 1])
    zb = zrcv[BACK, 0]
    for x in range(NXL):
        keep = (1 - W[x]).astype(jnp.float32)
        forward, back = [], []
        for c in range(3):
            v = step_scale * jnp.abs(V[c, x])
            side = S[c, x].astype(jnp.float32)
            forward.append(v * side)
            back.append(v * (1.0 - side))
        below_x = B[x]
        below_y = jnp.where(first_row, yrcv[BACK, 0, pl.ds(x, 1), :], pltpu.roll(back[1], 1, 0))
        below_z = jnp.where(first_lane, pltpu.roll(zb, (NZL - x) % NZL, 1), pltpu.roll(back[2], 1, 1))
        for s in range(SOL):
            k = s * NXL + x
            d = D[s, x + 1]
            yu, yl = y_pair(d, DIF, k)
            zu, zl = z_pair(d, zd, k)
            c0 = forward[0] + half_scale * (d + D[s, x + 2])
            c1 = below_x + half_scale * (d + D[s, x])
            if x == NXL - 1:
                c0 = c0 * up_x
            if x == 0:
                c1 = c1 * dn_x
            c2 = up_y * (forward[1] + half_scale * (d + yu))
            c3 = dn_y * (below_y + half_scale * (d + yl))
            c4 = up_z * (forward[2] + half_scale * (d + zu))
            c5 = dn_z * (below_z + half_scale * (d + zl))
            K[s, x] = keep * (1.0 - (((c0 + c1) + (c2 + c3)) + (c4 + c5)))
            for i, c in enumerate((c0, c1, c2, c3, c4, c5)):
                C[i, s, x] = keep * c

    def pack_coef(side):
        for k in range(SOL * NXL):
            c = C[2 + side, k // NXL, k % NXL]
            ysnd[COEF, side, pl.ds(k, 1), :] = c[NYL - 1:, :] if side == 0 else c[:1, :]

    both_far(pack_coef)

    PART = NXL // PARTS

    def out_copy(part):
        return pltpu.make_async_copy(
            A.at[STEPS, :, pl.ds(1 + part * PART, PART)], out_h.at[:, pl.ds(part * PART, PART)], out_sem.at[part]
        )

    for t in range(STEPS):
        for dim in range(3):
            wait_face(t, dim)

        if t % 2 == 0:
            def arrived(side):
                far_face(t, 1 - side).wait_recv()
                if t == 2:
                    far_face(COEF, 1 - side).wait_recv()
                if t > 0:
                    yrcv[t, 1 - side] = yrcv[t, 1 - side] + yrcv[COEF, 1 - side] * ysnd[t - 1, side]

            both_far(arrived)

        zr = (zrcv[t, 0], zrcv[t, 1])
        for x in range(NXL):
            for s in range(SOL):
                k = s * NXL + x
                a = A[t, s, x + 1]
                yu, yl = y_pair(a, t, k)
                zu, zl = z_pair(a, zr, k)
                new = (
                    (K[s, x] * a + C[0, s, x] * A[t, s, x + 2] + C[1, s, x] * A[t, s, x])
                    + (C[2, s, x] * yu + C[3, s, x] * yl)
                    + (C[4, s, x] * zu + C[5, s, x] * zl)
                )
                A[t + 1, s, x + 1] = new
                if t < STEPS - 1:
                    ysnd[t + 1, 0, pl.ds(k, 1), :] = new[NYL - 1:, :]
                    ysnd[t + 1, 1, pl.ds(k, 1), :] = new[:1, :]
            if t == STEPS - 1 and (x + 1) % PART == 0:
                out_copy(x // PART).start()

        if t % 2:
            def finish(side):
                far_face(t, 1 - side).wait_recv()
                rows = ysnd[t + 1, side] + ysnd[COEF, side] * late[t // 2]
                r = NYL - 1 if side == 0 else 0
                for k in range(SOL * NXL):
                    A[t + 1, k // NXL, k % NXL + 1, pl.ds(r, 1), :] = rows[k:k + 1, :]

            both_far(lambda side: far_face(t + 1, side).start())
            send_face(t + 1, 1)
            both_far(finish)

        if t < STEPS - 1:
            if t % 2 == 0:
                both_far(lambda side: far_face(t + 1, side).start())
            send_face(t + 1, 0)
            if t % 2 == 0:
                send_face(t + 1, 1)
            packs = no_packs()
            for k in range(SOL * NXL):
                packs = pack(packs, A[t + 1, k // NXL, k % NXL + 1], k)
            zsnd[t + 1, 0], zsnd[t + 1, 1] = packs
            send_face(t + 1, 2)
            if t == 0:
                both_far(lambda side: far_face(COEF, side).start())

    for m in range(STEPS):
        for dim in range(3):
            sent_face(m, dim)
    for dim in range(3):
        sent_face(DIF, dim)
        sent_face(BACK, dim, 0)

    def sent_far(side):
        for m in list(range(STEPS)) + [DIF, COEF]:
            far_face(m, side).wait_send()
        if side == 0:
            far_face(BACK, side).wait_send()

    both_far(sent_far)

    @pl.loop(1, group)
    def _(o):
        py, pz, p = peer(o)
        block(p, py, pz, me).wait_send()

        @pl.when(py == half)
        def _():
            edge(p, pz, me).wait_send()

    for part in range(PARTS):
        out_copy(part).wait()


def solution(mesh):
    counts = tuple(mesh.shape[a] for a in AXES)

    def local(adjoint_final, velocity, diffusivity, upwind_side, wall_mask):
        dims = adjoint_final.shape
        sol, nxl, nyl, nzl = dims
        f32 = jnp.float32
        group = counts[1] * counts[2]
        messages = STEPS + 4
        return pl.pallas_call(
            functools.partial(kernel, dims, counts),
            out_shape=jax.ShapeDtypeStruct(dims, f32),
            in_specs=[pl.BlockSpec(memory_space=pl.ANY)] * 5,
            out_specs=pl.BlockSpec(memory_space=pl.ANY),
            scratch_shapes=[
                pltpu.VMEM((STEPS + 1, sol, nxl + 2, nyl, nzl), f32),
                pltpu.VMEM((3, nxl, nyl, nzl), f32),
                pltpu.VMEM((sol, nxl + 2, nyl, nzl), f32),
                pltpu.VMEM((3, nxl, nyl, nzl), jnp.int32),
                pltpu.VMEM((nxl, nyl, nzl), jnp.int32),
                pltpu.VMEM((nxl + 1, nyl, nzl), f32),
                pltpu.VMEM((6, sol, nxl, nyl, nzl), f32),
                pltpu.VMEM((sol, nxl, nyl, nzl), f32),
                pltpu.VMEM((messages, 2, sol * nxl, nzl), f32),
                pltpu.VMEM((messages, 2, sol * nxl, nzl), f32),
                pltpu.VMEM((messages, 2, nyl, nzl), f32),
                pltpu.VMEM((messages, 2, nyl, nzl), f32),
                pltpu.VMEM((STEPS // 2, sol * nxl, nzl), f32),
                pltpu.VMEM((group, nyl, nzl), f32),
                pltpu.SemaphoreType.DMA((4,)),
                pltpu.SemaphoreType.DMA((group,)),
                pltpu.SemaphoreType.DMA((group,)),
                pltpu.SemaphoreType.DMA((group,)),
                pltpu.SemaphoreType.DMA((group,)),
                pltpu.SemaphoreType.DMA((messages, 3, 2)),
                pltpu.SemaphoreType.DMA((messages, 3, 2)),
                pltpu.SemaphoreType.DMA((PARTS,)),
            ],
            compiler_params=pltpu.CompilerParams(
                collective_id=0, has_side_effects=True, vmem_limit_bytes=62 << 20
            ),
        )(adjoint_final, velocity, diffusivity, upwind_side, wall_mask)

    return jax.shard_map(
        local,
        mesh=mesh,
        in_specs=(
            P(None, "gx", "gy", "gz"),
            P(None, ("gx", "gy", "gz"), None, None),
            P(None, "gx", "gy", "gz"),
            P(None, "gx", "gy", "gz"),
            P("gx", "gy", "gz"),
        ),
        out_specs=P(None, "gx", "gy", "gz"),
        check_vma=False,
    )
```
